32 devices in a mesh: group: 4 (over y, x), tile: 8 (over z, core).
Axes of the slice: x: 2, y: 2, z: 4, core: 2. Of those that a mesh axis runs over, the one named last changes fastest.
Arguments:
- frames: bfloat16 [12, 8, 32, 96, 256], P('group', None, 'tile'), may hold values from -6 to 6
- packing: int32 [12, 4], replicated, as said below
- w_space: bfloat16 [3, 3, 96, 96], replicated, may hold values from -0.21875 to 0.21875
- w_time: bfloat16 [3, 96, 96], replicated, may hold values from -0.375 to 0.375
- gain_one: float32 [96], replicated, may hold values from 0.1 to 1.9
- gain_two: float32 [96], replicated, may hold values from 0.1 to 1.9
Outputs:
- output: bfloat16 [12, 8, 32, 96, 256], P('group', None, 'tile')
The draws below stay inside these ranges and needn't reach their ends.
Inputs may be any that keep to these rules, and one draw needn't show every extreme that they name: `packing`: column 0 is 1 where the slot's span continues a clip and 0 for a clip's first span, whose other source fields are not read. `packing`: a span with a successor has 8 valid frames, so every preceding span is full; the slots of one device have their preceding spans on distinct devices.
All inputs are finite; a program needn't handle non-finite values.
Results may differ from the reference program's by a relative error of at most 0.004.
Values may be sent and summed in bfloat16 or wider, within the bound.
A program may use at most 192 MiB of HBM per device.

```python
import jax
import jax.numpy as jnp
from jax import lax

CHANNELS = 96
FRAMES = 8
SLOTS = 3
COLS = 256
SLOTS_ALL = 12
ROWS = 32


def draw_packing(key, part):
    span_count = SLOTS_ALL // SLOTS
    key_perm, key_head, key_count = jax.random.split(jax.random.fold_in(key, 7), 3)
    orders = jax.vmap(lambda sub: jax.random.permutation(sub, SLOTS))(jax.random.split(key_perm, span_count)).astype(jnp.int32)
    global_ids = jnp.arange(SLOTS_ALL, dtype=jnp.int32)
    device_of = global_ids // SLOTS
    slot_of = global_ids % SLOTS
    src_device = (device_of - 1 - slot_of) % span_count
    src_slot = orders[src_device, slot_of]
    previous = (src_device * SLOTS + src_slot).astype(jnp.int32)

    def lowest_step(turn_index, state):
        current, lowest = state
        current = previous[current]
        return (current, jnp.minimum(lowest, current))
    _, lowest = lax.fori_loop(0, SLOTS_ALL, lowest_step, (global_ids, global_ids))
    heads = (jax.random.randint(key_head, (SLOTS_ALL,), 0, 3) == 0) | (lowest == global_ids)
    successor = jnp.zeros((SLOTS_ALL,), jnp.int32).at[previous].set(global_ids)
    is_last = heads[successor]
    drawn = jax.random.randint(key_count, (SLOTS_ALL,), 1, FRAMES + 1)
    valid = jnp.where(is_last & (global_ids != 0), drawn, FRAMES)
    continues = jnp.where(heads, 0, 1).astype(jnp.int32)
    return jnp.stack([continues, valid, src_device, src_slot], axis=1).astype(jnp.int32)


def shard_levels(rng, shape, shards, smallest, top_value):
    level = 1.0
    for dim, shards_of in shards:
        steps = jax.random.uniform(jax.random.fold_in(jax.random.fold_in(rng, 6), dim), (shards_of,), jnp.float32, smallest / len(shards), top_value / len(shards))
        level = level * jnp.repeat(jnp.exp(steps), shape[dim] // shards_of).reshape((-1,) + (1,) * (len(shape) - 1 - dim))
    return level


def gaussian(key, extent, spread, limit, cuts=(), held_as=jnp.bfloat16):
    values = jax.random.normal(key, extent, jnp.float32) * spread
    if len(cuts) > 0:
        values = shard_levels(key, extent, cuts, -0.22, 0.18) * values
    return jnp.clip(values, min=-limit, max=limit).astype(held_as)


def setup_inputs(seed: int = 0) -> dict:
    key_list = jax.random.split(jax.random.key(seed), 7)
    return {
        "frames": gaussian(key_list[0], (SLOTS_ALL, FRAMES, ROWS, CHANNELS, COLS), 1.0, 6.0, ((0, 4), (2, 8))),
        "packing": draw_packing(jax.random.fold_in(key_list[6], 71), 0),
        "w_space": gaussian(key_list[2], (3, 3, CHANNELS, CHANNELS), (9 * CHANNELS) ** -0.5, 0.21875),
        "w_time": gaussian(key_list[3], (3, CHANNELS, CHANNELS), (3 * CHANNELS) ** -0.5, 0.375),
        "gain_one": jnp.clip(1.0 + 0.18 * jax.random.normal(key_list[4], (CHANNELS,), jnp.float32), 0.1, 1.9),
        "gain_two": jnp.clip(1.0 + 0.18 * jax.random.normal(key_list[5], (CHANNELS,), jnp.float32), 0.1, 1.9),
    }


def norm_act(values, gain_vec):
    meansq = lax.optimization_barrier(jnp.mean(values * values, axis=-2, keepdims=True))
    return jax.nn.silu(values * lax.rsqrt(meansq + 1e-06) * gain_vec[:, None])

def reference(frames, packing, w_space, w_time, gain_one, gain_two):
    space_f = w_space.astype(jnp.float32)
    time_f = w_time.astype(jnp.float32)

    def branch(slot_frames):
        hidden = norm_act(slot_frames.astype(jnp.float32), gain_one).astype(jnp.bfloat16)
        padded = jnp.pad(hidden.astype(jnp.float32), ((0, 0), (1, 1), (0, 0), (1, 1)))
        summed = jnp.zeros(slot_frames.shape, jnp.float32)
        for tap_row in range(3):
            for tap_col in range(3):
                window = padded[:, tap_row:tap_row + ROWS, :, tap_col:tap_col + COLS]
                summed = summed + jnp.einsum('oi,fyix->fyox', space_f[tap_row, tap_col], window, precision=lax.Precision.HIGHEST)
        return norm_act(summed, gain_two).astype(jnp.bfloat16)
    act = lax.map(branch, frames)
    tails = act[:, FRAMES - 2:]
    source = (packing[:, 2] * SLOTS + packing[:, 3]).astype(jnp.int32)
    has_prev = packing[:, 0] > 0
    cache = jnp.where(has_prev[:, None, None, None, None], tails[source], jnp.zeros_like(tails))

    def finish(items):
        slot_frames, slot_act, slot_cache, valid = items
        extended = jnp.concatenate([slot_cache, slot_act], axis=0).astype(jnp.float32)
        temporal = jnp.zeros(slot_frames.shape, jnp.float32)
        for tap in range(3):
            temporal = temporal + jnp.einsum('oi,fyix->fyox', time_f[tap], extended[tap:tap + FRAMES], precision=lax.Precision.HIGHEST)
        keep = jnp.arange(FRAMES) < valid
        result = jnp.where(keep[:, None, None, None], slot_frames.astype(jnp.float32) + temporal, 0.0)
        return result.astype(jnp.bfloat16)
    return lax.map(finish, (frames, act, cache, packing[:, 1]))
```

```python
import functools

import jax
import jax.numpy as jnp
from jax import lax
from jax.experimental import pallas as pl
from jax.experimental.pallas import tpu as pltpu
from jax.sharding import PartitionSpec as P

BF16 = jnp.bfloat16
F32 = jnp.float32


def norm_silu(values, half_gain):
    total = jnp.sum(values * values, axis=0, keepdims=True)
    scale = lax.rsqrt(total * (1.0 / values.shape[0]) + 1e-06)
    u = values * scale * half_gain
    return (u + u * jnp.tanh(u)).astype(BF16)


def kernel(
    packing, frames_hbm, w_space, w_time, gain_one, gain_two, out_hbm,
    x, hid, ext, send, recv, ws, wt, g1, g2,
    in_sem, out_sem, halo_send, halo_recv, tail_send, tail_recv,
):
    slots, frame_count, rows, chans, cols = x.shape
    pairs = frame_count // 2
    group_count, tile_count = lax.axis_size("group"), lax.axis_size("tile")
    me, tile = lax.axis_index("group"), lax.axis_index("tile")
    has_low, has_high = tile > 0, tile < tile_count - 1
    order = [pairs - 1] + list(range(pairs - 1))

    def fetch(pair):
        return pltpu.make_async_copy(
            frames_hbm.at[:, pl.ds(2 * pair, 2)], x.at[:, pl.ds(2 * pair, 2)], in_sem.at[pair]
        )

    for pair in order:
        fetch(pair).start()

    barrier = pltpu.get_barrier_semaphore()
    for off in range(1, group_count):
        pl.semaphore_signal(
            barrier, inc=1, device_id={"group": lax.rem(me + off, group_count)},
            device_id_type=pl.DeviceIdType.MESH,
        )

    @pl.when(has_low)
    def _():
        pl.semaphore_signal(
            barrier, inc=1, device_id={"tile": tile - 1}, device_id_type=pl.DeviceIdType.MESH
        )

    @pl.when(has_high)
    def _():
        pl.semaphore_signal(
            barrier, inc=1, device_id={"tile": tile + 1}, device_id_type=pl.DeviceIdType.MESH
        )

    for q in range(3):
        ws[q * chans : (q + 1) * chans, :] = jnp.concatenate(
            [w_space[p, q] for p in range(3)], axis=1
        )
    zero = jnp.zeros((chans, chans), BF16)
    taps = [w_time[k] for k in range(3)]
    wt[0:chans, :] = jnp.concatenate(taps + [zero], axis=1)
    wt[chans : 2 * chans, :] = jnp.concatenate([zero] + taps, axis=1)
    g1[...] = jnp.transpose(jnp.broadcast_to(gain_one[...] * 0.5, (cols, chans)))
    g2[...] = jnp.transpose(jnp.broadcast_to(gain_two[...] * 0.5, (cols, chans)))

    @pl.when(tile == 0)
    def _():
        hid[:, :, 0:chans, :] = jnp.zeros((slots, frame_count, chans, cols), BF16)

    @pl.when(tile == tile_count - 1)
    def _():
        hid[:, :, (rows + 1) * chans :, :] = jnp.zeros((slots, frame_count, chans, cols), BF16)

    def halo_up(pair):
        at = pl.ds(2 * pair, 2)
        return pltpu.make_async_remote_copy(
            src_ref=hid.at[:, at, pl.ds(rows * chans, chans)],
            dst_ref=hid.at[:, at, pl.ds(0, chans)],
            send_sem=halo_send.at[0, pair],
            recv_sem=halo_recv.at[0, pair],
            device_id={"tile": lax.rem(tile + 1, tile_count)},
            device_id_type=pl.DeviceIdType.MESH,
        )

    def halo_down(pair):
        at = pl.ds(2 * pair, 2)
        return pltpu.make_async_remote_copy(
            src_ref=hid.at[:, at, pl.ds(chans, chans)],
            dst_ref=hid.at[:, at, pl.ds((rows + 1) * chans, chans)],
            send_sem=halo_send.at[1, pair],
            recv_sem=halo_recv.at[1, pair],
            device_id={"tile": lax.rem(tile + tile_count - 1, tile_count)},
            device_id_type=pl.DeviceIdType.MESH,
        )

    def first_norm(pair, which):
        def step(i, carry):
            n, f = i // 2, 2 * pair + i % 2
            for y in which:
                values = x[n, f, y].astype(F32)
                hid[n, f, (y + 1) * chans : (y + 2) * chans, :] = norm_silu(values, g1[...])
            return carry

        lax.fori_loop(0, 2 * slots, step, 0)

    def send_halo(pair):
        pl.when(has_high)(lambda: halo_up(pair).start())
        pl.when(has_low)(lambda: halo_down(pair).start())

    def await_halo(pair):
        pl.when(has_low)(lambda: halo_up(pair).wait_recv())
        pl.when(has_high)(lambda: halo_down(pair).wait_recv())

    lane = lax.broadcasted_iota(jnp.int32, (chans, cols), 1)

    def conv_frame(n, f):
        for y in range(rows):
            prod = jnp.dot(
                ws[...], hid[n, f, y * chans : (y + 3) * chans, :], preferred_element_type=F32
            )
            low = jnp.where(lane == 0, 0.0, pltpu.roll(prod[0:chans], 1, 1))
            high = jnp.where(lane == cols - 1, 0.0, pltpu.roll(prod[2 * chans :], cols - 1, 1))
            spatial = prod[chans : 2 * chans] + low + high
            at = pl.multiple_of((f + 2) * chans, chans)
            ext[n, y, pl.ds(at, chans), :] = norm_silu(spatial, g2[...])

    def conv_slots(f):
        def step(n, carry):
            conv_frame(n, f)
            return carry

        lax.fori_loop(0, slots, step, 0)

    def tail(off, k):
        return pltpu.make_async_remote_copy(
            src_ref=send.at[off - 1, k],
            dst_ref=recv.at[off - 1, k],
            send_sem=tail_send.at[off - 1, k],
            recv_sem=tail_recv.at[off - 1, k],
            device_id={"group": lax.rem(me + off, group_count)},
            device_id_type=pl.DeviceIdType.MESH,
        )

    def send_tails(k):
        f = frame_count - 2 + k
        for off in range(1, group_count):
            dest = lax.rem(me + off, group_count)
            wanted = jnp.int32(0)
            for n in range(slots):
                entry = dest * slots + n
                match = (packing[entry, 0] > 0) & (packing[entry, 2] == me)
                wanted = jnp.where(match, packing[entry, 3], wanted)

            def step(y, carry):
                at = slice((f + 2) * chans, (f + 3) * chans)
                value = ext[0, y, at, :]
                for n in range(1, slots):
                    value = lax.select(wanted == n, ext[n, y, at, :], value)
                send[off - 1, k, y] = value
                return carry

            lax.fori_loop(0, rows, step, 0)
            tail(off, k).start()

    def temporal(n, y, pair):
        prod = jnp.dot(
            wt[...],
            ext[n, y, 2 * pair * chans : (2 * pair + 4) * chans, :],
            preferred_element_type=F32,
        )
        count = packing[me * slots + n, 1]
        for k in range(2):
            f = 2 * pair + k
            value = x[n, f, y].astype(F32) + prod[k * chans : (k + 1) * chans]
            x[n, f, y] = lax.select(f < count, value, jnp.zeros_like(value)).astype(BF16)

    last = pairs - 1
    fetch(last).wait()
    first_norm(last, (0, rows - 1))
    pl.semaphore_wait(
        barrier, group_count - 1 + has_low.astype(jnp.int32) + has_high.astype(jnp.int32)
    )
    send_halo(last)
    first_norm(last, range(1, rows - 1))
    fetch(0).wait()
    first_norm(0, range(rows))
    send_halo(0)
    await_halo(last)
    for k in range(2):
        conv_slots(frame_count - 2 + k)
        send_tails(k)
    for pair in range(1, last):
        fetch(pair).wait()
        first_norm(pair, range(rows))
        send_halo(pair)
    for pair in range(last):
        await_halo(pair)

        def conv_step(i, carry):
            conv_frame(i // 2, 2 * pair + i % 2)
            return carry

        lax.fori_loop(0, 2 * slots, conv_step, 0)

    def later_step(i, carry):
        for pair in range(1, pairs):
            temporal(i // rows, i % rows, pair)
        return carry

    lax.fori_loop(0, slots * rows, later_step, 0)
    out_late = pltpu.make_async_copy(
        x.at[:, pl.ds(2, frame_count - 2)], out_hbm.at[:, pl.ds(2, frame_count - 2)], out_sem.at[0]
    )
    out_late.start()

    for off in range(1, group_count):
        for k in range(2):
            tail(off, k).wait_recv()

    def first_step(i, carry):
        n, y = i // rows, i % rows
        entry = me * slots + n
        has_prev, source, slot = packing[entry, 0] > 0, packing[entry, 2], packing[entry, 3]
        for k in range(2):
            at = slice((frame_count + k) * chans, (frame_count + k + 1) * chans)
            value = jnp.zeros((chans, cols), BF16)
            for s in range(slots):
                own = has_prev & (source == me) & (slot == s)
                value = lax.select(own, ext[s, y, at, :], value)
            for off in range(1, group_count):
                sender = lax.rem(me + group_count - off, group_count)
                value = lax.select(has_prev & (source == sender), recv[off - 1, k, y], value)
            ext[n, y, k * chans : (k + 1) * chans, :] = value
        temporal(n, y, 0)
        return carry

    lax.fori_loop(0, slots * rows, first_step, 0)
    out_early = pltpu.make_async_copy(
        x.at[:, pl.ds(0, 2)], out_hbm.at[:, pl.ds(0, 2)], out_sem.at[1]
    )
    out_early.start()

    for off in range(1, group_count):
        for k in range(2):
            tail(off, k).wait_send()
    for pair in range(pairs):
        pl.when(has_high)(lambda: halo_up(pair).wait_send())
        pl.when(has_low)(lambda: halo_down(pair).wait_send())
    out_late.wait()
    out_early.wait()


def body(group_count, frames, packing, w_space, w_time, gain_one, gain_two):
    slots, frame_count, rows, chans, cols = frames.shape
    pairs = frame_count // 2
    vmem = pl.BlockSpec(memory_space=pltpu.VMEM)
    pixels = slots * frame_count * rows * cols
    return pl.pallas_call(
        kernel,
        out_shape=jax.ShapeDtypeStruct(frames.shape, BF16),
        in_specs=[
            pl.BlockSpec(memory_space=pltpu.SMEM),
            pl.BlockSpec(memory_space=pl.ANY),
            vmem, vmem, vmem, vmem,
        ],
        out_specs=pl.BlockSpec(memory_space=pl.ANY),
        scratch_shapes=[
            pltpu.VMEM(frames.shape, BF16),
            pltpu.VMEM((slots, frame_count, (rows + 2) * chans, cols), BF16),
            pltpu.VMEM((slots, rows, (frame_count + 2) * chans, cols), BF16),
            pltpu.VMEM((group_count - 1, 2, rows, chans, cols), BF16),
            pltpu.VMEM((group_count - 1, 2, rows, chans, cols), BF16),
            pltpu.VMEM((3 * chans, 3 * chans), BF16),
            pltpu.VMEM((2 * chans, 4 * chans), BF16),
            pltpu.VMEM((chans, cols), F32),
            pltpu.VMEM((chans, cols), F32),
            pltpu.SemaphoreType.DMA((pairs,)),
            pltpu.SemaphoreType.DMA((2,)),
            pltpu.SemaphoreType.DMA((2, pairs)),
            pltpu.SemaphoreType.DMA((2, pairs)),
            pltpu.SemaphoreType.DMA((group_count - 1, 2)),
            pltpu.SemaphoreType.DMA((group_count - 1, 2)),
        ],
        cost_estimate=pl.CostEstimate(
            flops=24 * chans * chans * pixels,
            bytes_accessed=4 * chans * pixels,
            transcendentals=2 * chans * pixels,
        ),
        compiler_params=pltpu.CompilerParams(
            collective_id=0, has_side_effects=True, vmem_limit_bytes=48 * 1024 * 1024
        ),
    )(packing, frames, w_space, w_time, gain_one[None, :], gain_two[None, :])


def solution(mesh):
    in_specs = (P("group", None, "tile", None, None), P(), P(), P(), P(), P())
    out_specs = P("group", None, "tile", None, None)
    return jax.shard_map(
        functools.partial(body, mesh.shape["group"]),
        mesh=mesh, in_specs=in_specs, out_specs=out_specs, check_vma=False,
    )
```

```python
import functools

import jax
import jax.numpy as jnp
from jax import lax
from jax.experimental import pallas as pl
from jax.experimental.pallas import tpu as pltpu
from jax.sharding import PartitionSpec as P

BF16 = jnp.bfloat16
F32 = jnp.float32


def norm_silu(values, half_gain):
    total = jnp.sum(values * values, axis=0, keepdims=True)
    scale = lax.rsqrt(total * (1.0 / values.shape[0]) + 1e-06)
    u = values * scale * half_gain
    return (u + u * jnp.tanh(u)).astype(BF16)


def kernel(
    packing_hbm, frames_hbm, w_space_hbm, w_time_hbm, gain_one_hbm, gain_two_hbm, out_hbm,
    packing, w_space, w_time, gain_one, gain_two,
    x, hid, ext, send, recv, ws, wt, g1, g2,
    in_sem, small_sem, out_sem, halo_send, halo_recv, tail_send, tail_recv,
):
    slots, frame_count, rows, chans, cols = x.shape
    pairs = frame_count // 2
    group_count, tile_count = lax.axis_size("group"), lax.axis_size("tile")
    me, tile = lax.axis_index("group"), lax.axis_index("tile")
    has_low, has_high = tile > 0, tile < tile_count - 1
    order = [pairs - 1] + list(range(pairs - 1))

    def fetch(pair):
        return pltpu.make_async_copy(
            frames_hbm.at[:, pl.ds(2 * pair, 2)], x.at[:, pl.ds(2 * pair, 2)], in_sem.at[pair]
        )

    small = [
        pltpu.make_async_copy(src, dst, small_sem.at[i])
        for i, (src, dst) in enumerate(
            [
                (gain_one_hbm, gain_one), (packing_hbm, packing), (w_space_hbm, w_space),
                (gain_two_hbm, gain_two), (w_time_hbm, w_time),
            ]
        )
    ]
    small[0].start()
    fetch(order[0]).start()
    for copy in small[1:]:
        copy.start()
    for pair in order[1:]:
        fetch(pair).start()

    barrier = pltpu.get_barrier_semaphore()
    for off in range(1, group_count):
        pl.semaphore_signal(
            barrier, inc=1, device_id={"group": lax.rem(me + off, group_count)},
            device_id_type=pl.DeviceIdType.MESH,
        )

    @pl.when(has_low)
    def _():
        pl.semaphore_signal(
            barrier, inc=1, device_id={"tile": tile - 1}, device_id_type=pl.DeviceIdType.MESH
        )

    @pl.when(has_high)
    def _():
        pl.semaphore_signal(
            barrier, inc=1, device_id={"tile": tile + 1}, device_id_type=pl.DeviceIdType.MESH
        )

    def expand_gain(gain):
        return jnp.transpose(jnp.broadcast_to(gain[...] * 0.5, (cols, chans)))

    @pl.when(tile == 0)
    def _():
        hid[:, :, 0:chans, :] = jnp.zeros((slots, frame_count, chans, cols), BF16)

    @pl.when(tile == tile_count - 1)
    def _():
        hid[:, :, (rows + 1) * chans :, :] = jnp.zeros((slots, frame_count, chans, cols), BF16)

    def halo_up(pair):
        at = pl.ds(2 * pair, 2)
        return pltpu.make_async_remote_copy(
            src_ref=hid.at[:, at, pl.ds(rows * chans, chans)],
            dst_ref=hid.at[:, at, pl.ds(0, chans)],
            send_sem=halo_send.at[0, pair],
            recv_sem=halo_recv.at[0, pair],
            device_id={"tile": lax.rem(tile + 1, tile_count)},
            device_id_type=pl.DeviceIdType.MESH,
        )

    def halo_down(pair):
        at = pl.ds(2 * pair, 2)
        return pltpu.make_async_remote_copy(
            src_ref=hid.at[:, at, pl.ds(chans, chans)],
            dst_ref=hid.at[:, at, pl.ds((rows + 1) * chans, chans)],
            send_sem=halo_send.at[1, pair],
            recv_sem=halo_recv.at[1, pair],
            device_id={"tile": lax.rem(tile + tile_count - 1, tile_count)},
            device_id_type=pl.DeviceIdType.MESH,
        )

    def first_norm(pair, which):
        def step(i, carry):
            n, f = i // 2, 2 * pair + i % 2
            for y in which:
                values = x[n, f, y].astype(F32)
                hid[n, f, (y + 1) * chans : (y + 2) * chans, :] = norm_silu(values, g1[...])
            return carry

        lax.fori_loop(0, 2 * slots, step, 0)

    def send_halo(pair):
        pl.when(has_high)(lambda: halo_up(pair).start())
        pl.when(has_low)(lambda: halo_down(pair).start())

    def await_halo(pair):
        pl.when(has_low)(lambda: halo_up(pair).wait_recv())
        pl.when(has_high)(lambda: halo_down(pair).wait_recv())

    lane = lax.broadcasted_iota(jnp.int32, (chans, cols), 1)

    def conv_rows(n, f, which):
        for y in which:
            prod = jnp.dot(
                ws[...], hid[n, f, y * chans : (y + 3) * chans, :], preferred_element_type=F32
            )
            low = jnp.where(lane == 0, 0.0, pltpu.roll(prod[0:chans], 1, 1))
            high = jnp.where(lane == cols - 1, 0.0, pltpu.roll(prod[2 * chans :], cols - 1, 1))
            spatial = prod[chans : 2 * chans] + low + high
            at = pl.multiple_of((f + 2) * chans, chans)
            ext[n, y, pl.ds(at, chans), :] = norm_silu(spatial, g2[...])

    blocks = [(1, rows - 2), (0, 1), (rows - 1, 1)]

    def tail(off, piece):
        k, (low, size) = piece % 2, blocks[piece // 2]
        return pltpu.make_async_remote_copy(
            src_ref=send.at[off - 1, k, pl.ds(low, size)],
            dst_ref=recv.at[off - 1, k, pl.ds(low, size)],
            send_sem=tail_send.at[off - 1, piece],
            recv_sem=tail_recv.at[off - 1, piece],
            device_id={"group": lax.rem(me + off, group_count)},
            device_id_type=pl.DeviceIdType.MESH,
        )

    def send_tails(piece):
        k, (low, size) = piece % 2, blocks[piece // 2]
        f = frame_count - 2 + k
        at = slice((f + 2) * chans, (f + 3) * chans)
        for off in range(1, group_count):
            dest = lax.rem(me + off, group_count)
            wanted = jnp.int32(0)
            for n in range(slots):
                entry = dest * slots + n
                match = (packing[0, entry] > 0) & (packing[2, entry] == me)
                wanted = jnp.where(match, packing[3, entry], wanted)
            for y in range(low, low + size):
                value = ext[0, y, at, :]
                for n in range(1, slots):
                    value = lax.select(wanted == n, ext[n, y, at, :], value)
                send[off - 1, k, y] = value
            tail(off, piece).start()

    def temporal(n, y, pair):
        prod = jnp.dot(
            wt[...],
            ext[n, y, 2 * pair * chans : (2 * pair + 4) * chans, :],
            preferred_element_type=F32,
        )
        count = packing[1, me * slots + n]
        for k in range(2):
            f = 2 * pair + k
            value = x[n, f, y].astype(F32) + prod[k * chans : (k + 1) * chans]
            x[n, f, y] = lax.select(f < count, value, jnp.zeros_like(value)).astype(BF16)

    stores = []

    def store(pair, low, size):
        at = (slice(None), pl.ds(2 * pair, 2), pl.ds(low, size))
        copy = pltpu.make_async_copy(x.at[at], out_hbm.at[at], out_sem.at[len(stores)])
        stores.append(copy)
        copy.start()

    def tail_rows(piece):
        k, (low, size) = piece % 2, blocks[piece // 2]

        def step(n, carry):
            conv_rows(n, frame_count - 2 + k, range(low, low + size))
            return carry

        lax.fori_loop(0, slots, step, 0)
        send_tails(piece)

    last = pairs - 1
    small[0].wait()
    g1[...] = expand_gain(gain_one)
    fetch(last).wait()
    first_norm(last, (0, rows - 1))
    pl.semaphore_wait(
        barrier, group_count - 1 + has_low.astype(jnp.int32) + has_high.astype(jnp.int32)
    )
    send_halo(last)
    first_norm(last, range(1, rows - 1))
    for copy in small[1:]:
        copy.wait()
    for q in range(3):
        ws[q * chans : (q + 1) * chans, :] = jnp.concatenate(
            [w_space[p, q] for p in range(3)], axis=1
        )
    zero = jnp.zeros((chans, chans), BF16)
    taps = [w_time[k] for k in range(3)]
    wt[0:chans, :] = jnp.concatenate(taps + [zero], axis=1)
    wt[chans : 2 * chans, :] = jnp.concatenate([zero] + taps, axis=1)
    g2[...] = expand_gain(gain_two)
    tail_rows(0)
    tail_rows(1)
    fetch(0).wait()
    first_norm(0, range(rows))
    send_halo(0)
    await_halo(last)
    for piece in range(2, 6):
        tail_rows(piece)
    for pair in range(1, last):
        fetch(pair).wait()
        first_norm(pair, range(rows))
        send_halo(pair)
    for pair in range(pairs):
        if pair < last:
            await_halo(pair)

        def step(n, carry):
            if pair < last:
                for k in range(2):
                    conv_rows(n, 2 * pair + k, range(rows))
            if pair > 0:
                for y in range(rows):
                    temporal(n, y, pair)
            return carry

        lax.fori_loop(0, slots, step, 0)
        if pair > 0:
            store(pair, 0, rows)

    for block, (low, size) in enumerate(blocks):
        for off in range(1, group_count):
            for k in range(2):
                tail(off, 2 * block + k).wait_recv()

        def first_step(n, carry):
            entry = me * slots + n
            has_prev, source, slot = packing[0, entry] > 0, packing[2, entry], packing[3, entry]
            for y in range(low, low + size):
                for k in range(2):
                    at = slice((frame_count + k) * chans, (frame_count + k + 1) * chans)
                    value = jnp.zeros((chans, cols), BF16)
                    for s in range(slots):
                        own = has_prev & (source == me) & (slot == s)
                        value = lax.select(own, ext[s, y, at, :], value)
                    for off in range(1, group_count):
                        sender = lax.rem(me + group_count - off, group_count)
                        theirs = has_prev & (source == sender)
                        value = lax.select(theirs, recv[off - 1, k, y], value)
                    ext[n, y, k * chans : (k + 1) * chans, :] = value
                temporal(n, y, 0)
            return carry

        lax.fori_loop(0, slots, first_step, 0)
        store(0, low, size)

    for off in range(1, group_count):
        for piece in range(6):
            tail(off, piece).wait_send()
    for pair in range(pairs):
        pl.when(has_high)(lambda: halo_up(pair).wait_send())
        pl.when(has_low)(lambda: halo_down(pair).wait_send())
    for copy in stores:
        copy.wait()


def body(group_count, frames, packing, w_space, w_time, gain_one, gain_two):
    slots, frame_count, rows, chans, cols = frames.shape
    pairs = frame_count // 2
    pixels = slots * frame_count * rows * cols
    return pl.pallas_call(
        kernel,
        out_shape=jax.ShapeDtypeStruct(frames.shape, BF16),
        in_specs=[
            pl.BlockSpec(memory_space=pltpu.HBM) for _ in range(6)
        ],
        out_specs=pl.BlockSpec(memory_space=pltpu.HBM),
        scratch_shapes=[
            pltpu.SMEM(packing.shape[::-1], jnp.int32),
            pltpu.VMEM(w_space.shape, BF16),
            pltpu.VMEM(w_time.shape, BF16),
            pltpu.VMEM((1, chans), F32),
            pltpu.VMEM((1, chans), F32),
            pltpu.VMEM(frames.shape, BF16),
            pltpu.VMEM((slots, frame_count, (rows + 2) * chans, cols), BF16),
            pltpu.VMEM((slots, rows, (frame_count + 2) * chans, cols), BF16),
            pltpu.VMEM((group_count - 1, 2, rows, chans, cols), BF16),
            pltpu.VMEM((group_count - 1, 2, rows, chans, cols), BF16),
            pltpu.VMEM((3 * chans, 3 * chans), BF16),
            pltpu.VMEM((2 * chans, 4 * chans), BF16),
            pltpu.VMEM((chans, cols), F32),
            pltpu.VMEM((chans, cols), F32),
            pltpu.SemaphoreType.DMA((pairs,)),
            pltpu.SemaphoreType.DMA((5,)),
            pltpu.SemaphoreType.DMA((pairs + 2,)),
            pltpu.SemaphoreType.DMA((2, pairs)),
            pltpu.SemaphoreType.DMA((2, pairs)),
            pltpu.SemaphoreType.DMA((group_count - 1, 6)),
            pltpu.SemaphoreType.DMA((group_count - 1, 6)),
        ],
        cost_estimate=pl.CostEstimate(
            flops=24 * chans * chans * pixels,
            bytes_accessed=4 * chans * pixels,
            transcendentals=2 * chans * pixels,
        ),
        compiler_params=pltpu.CompilerParams(
            collective_id=0, has_side_effects=True, vmem_limit_bytes=59 * 1024 * 1024
        ),
    )(packing.T, frames, w_space, w_time, gain_one[None, :], gain_two[None, :])


def solution(mesh):
    in_specs = (P("group", None, "tile", None, None), P(), P(), P(), P(), P())
    out_specs = P("group", None, "tile", None, None)
    return jax.shard_map(
        functools.partial(body, mesh.shape["group"]),
        mesh=mesh, in_specs=in_specs, out_specs=out_specs, check_vma=False,
    )
```

```python
import functools

import jax
import jax.numpy as jnp
from jax import lax
from jax.experimental import pallas as pl
from jax.experimental.pallas import tpu as pltpu
from jax.sharding import PartitionSpec as P

BF16 = jnp.bfloat16
F32 = jnp.float32


def norm_silu(values, half_gain):
    total = jnp.sum(values * values, axis=0, keepdims=True)
    scale = lax.rsqrt(total * (1.0 / values.shape[0]) + 1e-06)
    u = values * scale * half_gain
    return (u + u * jnp.tanh(u)).astype(BF16)


def kernel(
    packing_hbm, frames_hbm, w_space_hbm, w_time_hbm, gain_one_hbm, gain_two_hbm, out,
    packing, w_space, w_time, gain_one, gain_two,
    x, hid, ext, send, recv, ws, wt, g1, g2,
    in_sem, small_sem, halo_send, halo_recv, tail_send, tail_recv,
):
    slots, frame_count, rows, chans, cols = x.shape
    pairs = frame_count // 2
    group_count, tile_count = lax.axis_size("group"), lax.axis_size("tile")
    me, tile = lax.axis_index("group"), lax.axis_index("tile")
    has_low, has_high = tile > 0, tile < tile_count - 1
    order = [pairs - 1] + list(range(pairs - 1))

    def fetch(pair):
        return pltpu.make_async_copy(
            frames_hbm.at[:, pl.ds(2 * pair, 2)], x.at[:, pl.ds(2 * pair, 2)], in_sem.at[pair]
        )

    small = [
        pltpu.make_async_copy(src, dst, small_sem.at[i])
        for i, (src, dst) in enumerate(
            [
                (gain_one_hbm, gain_one), (packing_hbm, packing), (w_space_hbm, w_space),
                (gain_two_hbm, gain_two), (w_time_hbm, w_time),
            ]
        )
    ]
    for copy in small[:4]:
        copy.start()
    for pair in order:
        fetch(pair).start()
    small[4].start()

    barrier = pltpu.get_barrier_semaphore()
    for off in range(1, group_count):
        pl.semaphore_signal(
            barrier, inc=1, device_id={"group": lax.rem(me + off, group_count)},
            device_id_type=pl.DeviceIdType.MESH,
        )

    @pl.when(has_low)
    def _():
        pl.semaphore_signal(
            barrier, inc=1, device_id={"tile": tile - 1}, device_id_type=pl.DeviceIdType.MESH
        )

    @pl.when(has_high)
    def _():
        pl.semaphore_signal(
            barrier, inc=1, device_id={"tile": tile + 1}, device_id_type=pl.DeviceIdType.MESH
        )

    def expand_gain(gain):
        return jnp.transpose(jnp.broadcast_to(gain[...] * 0.5, (cols, chans)))

    @pl.when(tile == 0)
    def _():
        hid[:, :, 0:chans, :] = jnp.zeros((slots, frame_count, chans, cols), BF16)

    @pl.when(tile == tile_count - 1)
    def _():
        hid[:, :, (rows + 1) * chans :, :] = jnp.zeros((slots, frame_count, chans, cols), BF16)

    def halo_up(pair):
        at = pl.ds(2 * pair, 2)
        return pltpu.make_async_remote_copy(
            src_ref=hid.at[:, at, pl.ds(rows * chans, chans)],
            dst_ref=hid.at[:, at, pl.ds(0, chans)],
            send_sem=halo_send.at[0, pair],
            recv_sem=halo_recv.at[0, pair],
            device_id={"tile": lax.rem(tile + 1, tile_count)},
            device_id_type=pl.DeviceIdType.MESH,
        )

    def halo_down(pair):
        at = pl.ds(2 * pair, 2)
        return pltpu.make_async_remote_copy(
            src_ref=hid.at[:, at, pl.ds(chans, chans)],
            dst_ref=hid.at[:, at, pl.ds((rows + 1) * chans, chans)],
            send_sem=halo_send.at[1, pair],
            recv_sem=halo_recv.at[1, pair],
            device_id={"tile": lax.rem(tile + tile_count - 1, tile_count)},
            device_id_type=pl.DeviceIdType.MESH,
        )

    def norm_frame(n, f, which):
        for y in which:
            values = x[n, f, y].astype(F32)
            hid[n, f, (y + 1) * chans : (y + 2) * chans, :] = norm_silu(values, g1[...])

    def norm_slots(f, which):
        def step(n, carry):
            norm_frame(n, f, which)
            return carry

        lax.fori_loop(0, slots, step, 0)

    def send_halo(pair):
        pl.when(has_high)(lambda: halo_up(pair).start())
        pl.when(has_low)(lambda: halo_down(pair).start())

    def await_halo(pair):
        pl.when(has_low)(lambda: halo_up(pair).wait_recv())
        pl.when(has_high)(lambda: halo_down(pair).wait_recv())

    lane = lax.broadcasted_iota(jnp.int32, (chans, cols), 1)

    def conv_rows(n, f, which):
        for y in which:
            prod = jnp.dot(
                ws[...], hid[n, f, y * chans : (y + 3) * chans, :], preferred_element_type=F32
            )
            low = jnp.where(lane == 0, 0.0, pltpu.roll(prod[0:chans], 1, 1))
            high = jnp.where(lane == cols - 1, 0.0, pltpu.roll(prod[2 * chans :], cols - 1, 1))
            spatial = prod[chans : 2 * chans] + low + high
            at = pl.multiple_of((f + 2) * chans, chans)
            ext[n, y, pl.ds(at, chans), :] = norm_silu(spatial, g2[...])

    blocks = [(1, rows - 2), (0, 1), (rows - 1, 1)]

    def tail(off, piece):
        k, (low, size) = piece % 2, blocks[piece // 2]
        return pltpu.make_async_remote_copy(
            src_ref=send.at[off - 1, k, pl.ds(low, size)],
            dst_ref=recv.at[off - 1, k, pl.ds(low, size)],
            send_sem=tail_send.at[off - 1, piece],
            recv_sem=tail_recv.at[off - 1, piece],
            device_id={"group": lax.rem(me + off, group_count)},
            device_id_type=pl.DeviceIdType.MESH,
        )

    def send_tails(piece):
        k, (low, size) = piece % 2, blocks[piece // 2]
        f = frame_count - 2 + k
        at = slice((f + 2) * chans, (f + 3) * chans)
        for off in range(1, group_count):
            dest = lax.rem(me + off, group_count)
            wanted = jnp.int32(0)
            for n in range(slots):
                entry = dest * slots + n
                match = (packing[0, entry] > 0) & (packing[2, entry] == me)
                wanted = jnp.where(match, packing[3, entry], wanted)
            for y in range(low, low + size):
                value = ext[0, y, at, :]
                for n in range(1, slots):
                    value = lax.select(wanted == n, ext[n, y, at, :], value)
                send[off - 1, k, y] = value
            tail(off, piece).start()

    def temporal(n, y, pair):
        prod = jnp.dot(
            wt[...],
            ext[n, y, 2 * pair * chans : (2 * pair + 4) * chans, :],
            preferred_element_type=F32,
        )
        count = packing[1, me * slots + n]
        for k in range(2):
            f = 2 * pair + k
            value = x[n, f, y].astype(F32) + prod[k * chans : (k + 1) * chans]
            out[n, f, y] = lax.select(f < count, value, jnp.zeros_like(value)).astype(BF16)

    def tail_rows(piece, norms):
        k, (low, size) = piece % 2, blocks[piece // 2]

        def step(n, carry):
            conv_rows(n, frame_count - 2 + k, range(low, low + size))
            for f in norms:
                norm_frame(n, f, range(rows))
            return carry

        lax.fori_loop(0, slots, step, 0)
        send_tails(piece)

    last = pairs - 1
    for copy in small[:4]:
        copy.wait()
    g1[...] = expand_gain(gain_one)
    g2[...] = expand_gain(gain_two)
    for q in range(3):
        ws[q * chans : (q + 1) * chans, :] = jnp.concatenate(
            [w_space[p, q] for p in range(3)], axis=1
        )
    fetch(last).wait()
    norm_slots(frame_count - 2, range(rows))
    pl.semaphore_wait(
        barrier, group_count - 1 + has_low.astype(jnp.int32) + has_high.astype(jnp.int32)
    )
    tail_rows(0, [])
    norm_slots(frame_count - 1, range(rows))
    send_halo(last)
    fetch(0).wait()
    tail_rows(1, [0, 1])
    send_halo(0)
    small[4].wait()
    zero = jnp.zeros((chans, chans), BF16)
    taps = [w_time[k] for k in range(3)]
    wt[0:chans, :] = jnp.concatenate(taps + [zero], axis=1)
    wt[chans : 2 * chans, :] = jnp.concatenate([zero] + taps, axis=1)
    await_halo(last)
    for pair in range(1, last):
        fetch(pair).wait()
    rest = list(range(2, frame_count - 2))
    share = -(-len(rest) // 4)
    for i in range(4):
        tail_rows(2 + i, rest[i * share : (i + 1) * share])
        for f in rest[i * share : (i + 1) * share]:
            if f % 2:
                send_halo(f // 2)
    for pair in range(pairs):
        if pair < last:
            await_halo(pair)

        def step(n, carry):
            if pair < last:
                for k in range(2):
                    conv_rows(n, 2 * pair + k, range(rows))
            if pair > 0:
                for y in range(rows):
                    temporal(n, y, pair)
            return carry

        lax.fori_loop(0, slots, step, 0)

    for block, (low, size) in enumerate(blocks):
        for off in range(1, group_count):
            for k in range(2):
                tail(off, 2 * block + k).wait_recv()

        def first_step(n, carry):
            entry = me * slots + n
            has_prev, source, slot = packing[0, entry] > 0, packing[2, entry], packing[3, entry]
            for y in range(low, low + size):
                for k in range(2):
                    at = slice((frame_count + k) * chans, (frame_count + k + 1) * chans)
                    value = jnp.zeros((chans, cols), BF16)
                    for s in range(slots):
                        own = has_prev & (source == me) & (slot == s)
                        value = lax.select(own, ext[s, y, at, :], value)
                    for off in range(1, group_count):
                        sender = lax.rem(me + group_count - off, group_count)
                        theirs = has_prev & (source == sender)
                        value = lax.select(theirs, recv[off - 1, k, y], value)
                    ext[n, y, k * chans : (k + 1) * chans, :] = value
                temporal(n, y, 0)
            return carry

        lax.fori_loop(0, slots, first_step, 0)

    for off in range(1, group_count):
        for piece in range(6):
            tail(off, piece).wait_send()
    for pair in range(pairs):
        pl.when(has_high)(lambda: halo_up(pair).wait_send())
        pl.when(has_low)(lambda: halo_down(pair).wait_send())


def body(group_count, frames, packing, w_space, w_time, gain_one, gain_two):
    slots, frame_count, rows, chans, cols = frames.shape
    pairs = frame_count // 2
    pixels = slots * frame_count * rows * cols
    return pl.pallas_call(
        kernel,
        out_shape=pltpu.VMEM(frames.shape, BF16),
        in_specs=[
            pl.BlockSpec(memory_space=pltpu.HBM) for _ in range(6)
        ],
        out_specs=pl.BlockSpec(memory_space=pltpu.VMEM),
        scratch_shapes=[
            pltpu.SMEM(packing.shape[::-1], jnp.int32),
            pltpu.VMEM(w_space.shape, BF16),
            pltpu.VMEM(w_time.shape, BF16),
            pltpu.VMEM((1, chans), F32),
            pltpu.VMEM((1, chans), F32),
            pltpu.VMEM(frames.shape, BF16),
            pltpu.VMEM((slots, frame_count, (rows + 2) * chans, cols), BF16),
            pltpu.VMEM((slots, rows, (frame_count + 2) * chans, cols), BF16),
            pltpu.VMEM((group_count - 1, 2, rows, chans, cols), BF16),
            pltpu.VMEM((group_count - 1, 2, rows, chans, cols), BF16),
            pltpu.VMEM((3 * chans, 3 * chans), BF16),
            pltpu.VMEM((2 * chans, 4 * chans), BF16),
            pltpu.VMEM((chans, cols), F32),
            pltpu.VMEM((chans, cols), F32),
            pltpu.SemaphoreType.DMA((pairs,)),
            pltpu.SemaphoreType.DMA((5,)),
            pltpu.SemaphoreType.DMA((2, pairs)),
            pltpu.SemaphoreType.DMA((2, pairs)),
            pltpu.SemaphoreType.DMA((group_count - 1, 6)),
            pltpu.SemaphoreType.DMA((group_count - 1, 6)),
        ],
        cost_estimate=pl.CostEstimate(
            flops=24 * chans * chans * pixels,
            bytes_accessed=4 * chans * pixels,
            transcendentals=2 * chans * pixels,
        ),
        compiler_params=pltpu.CompilerParams(
            collective_id=0, has_side_effects=True, vmem_limit_bytes=54 * 1024 * 1024
        ),
    )(packing.T, frames, w_space, w_time, gain_one[None, :], gain_two[None, :])


def solution(mesh):
    in_specs = (P("group", None, "tile", None, None), P(), P(), P(), P(), P())
    out_specs = P("group", None, "tile", None, None)
    return jax.shard_map(
        functools.partial(body, mesh.shape["group"]),
        mesh=mesh, in_specs=in_specs, out_specs=out_specs, check_vma=False,
    )
```

```python
import functools

import jax
import jax.numpy as jnp
from jax import lax
from jax.experimental import pallas as pl
from jax.experimental.pallas import tpu as pltpu
from jax.sharding import PartitionSpec as P

BF16 = jnp.bfloat16
F32 = jnp.float32


STRIP = 16


def silu_of_half(u):
    return (u + u * jnp.tanh(u)).astype(BF16)


def inverse_rms(squares, chans):
    return lax.rsqrt(jnp.sum(squares, axis=0, keepdims=True) * (1.0 / chans) + 1e-06)


def kernel(
    packing_hbm, frames_hbm, w_space_hbm, w_time_hbm, gain_one_hbm, gain_two_hbm, out,
    packing, w_space, w_time, gain_one, gain_two,
    x, hid, ext, send, recv, ws, wt, g1, g2, spat,
    in_sem, small_sem, halo_send, halo_recv, tail_send, tail_recv,
):
    slots, frame_count, rows, chans, cols = x.shape
    pairs = frame_count // 2
    group_count, tile_count = lax.axis_size("group"), lax.axis_size("tile")
    me, tile = lax.axis_index("group"), lax.axis_index("tile")
    has_low, has_high = tile > 0, tile < tile_count - 1
    order = [pairs - 1] + list(range(pairs - 1))

    def fetch(pair):
        return pltpu.make_async_copy(
            frames_hbm.at[:, pl.ds(2 * pair, 2)], x.at[:, pl.ds(2 * pair, 2)], in_sem.at[pair]
        )

    small = [
        pltpu.make_async_copy(src, dst, small_sem.at[i])
        for i, (src, dst) in enumerate(
            [
                (gain_one_hbm, gain_one), (packing_hbm, packing), (w_space_hbm, w_space),
                (gain_two_hbm, gain_two), (w_time_hbm, w_time),
            ]
        )
    ]
    for copy in small[:4]:
        copy.start()
    for pair in order:
        fetch(pair).start()
    small[4].start()

    barrier = pltpu.get_barrier_semaphore()
    for off in range(1, group_count):
        pl.semaphore_signal(
            barrier, inc=1, device_id={"group": lax.rem(me + off, group_count)},
            device_id_type=pl.DeviceIdType.MESH,
        )

    @pl.when(has_low)
    def _():
        pl.semaphore_signal(
            barrier, inc=1, device_id={"tile": tile - 1}, device_id_type=pl.DeviceIdType.MESH
        )

    @pl.when(has_high)
    def _():
        pl.semaphore_signal(
            barrier, inc=1, device_id={"tile": tile + 1}, device_id_type=pl.DeviceIdType.MESH
        )

    def expand_gain(gain):
        return jnp.transpose(jnp.broadcast_to(gain[...] * 0.5, (cols, chans)))

    @pl.when(tile == 0)
    def _():
        hid[:, :, 0:chans, :] = jnp.zeros((slots, frame_count, chans, cols), BF16)

    @pl.when(tile == tile_count - 1)
    def _():
        hid[:, :, (rows + 1) * chans :, :] = jnp.zeros((slots, frame_count, chans, cols), BF16)

    def halo_up(pair):
        at = pl.ds(2 * pair, 2)
        return pltpu.make_async_remote_copy(
            src_ref=hid.at[:, at, pl.ds(rows * chans, chans)],
            dst_ref=hid.at[:, at, pl.ds(0, chans)],
            send_sem=halo_send.at[0, pair],
            recv_sem=halo_recv.at[0, pair],
            device_id={"tile": lax.rem(tile + 1, tile_count)},
            device_id_type=pl.DeviceIdType.MESH,
        )

    def halo_down(pair):
        at = pl.ds(2 * pair, 2)
        return pltpu.make_async_remote_copy(
            src_ref=hid.at[:, at, pl.ds(chans, chans)],
            dst_ref=hid.at[:, at, pl.ds((rows + 1) * chans, chans)],
            send_sem=halo_send.at[1, pair],
            recv_sem=halo_recv.at[1, pair],
            device_id={"tile": lax.rem(tile + tile_count - 1, tile_count)},
            device_id_type=pl.DeviceIdType.MESH,
        )

    strips = [slice(low, low + STRIP) for low in range(0, chans, STRIP)]

    def norm_frame(n, f, which):
        scales = {}
        for y in which:
            squares = jnp.zeros((STRIP, cols), F32)
            for at in strips:
                values = x[n, f, y, at, :].astype(F32)
                squares += values * values
            scales[y] = inverse_rms(squares, chans)
        for y in which:
            for at in strips:
                u = x[n, f, y, at, :].astype(F32) * scales[y] * g1[at, :]
                low = (y + 1) * chans + at.start
                hid[n, f, low : low + STRIP, :] = silu_of_half(u)

    def norm_slots(f, which):
        def step(n, carry):
            norm_frame(n, f, which)
            return carry

        lax.fori_loop(0, slots, step, 0)

    def send_halo(pair):
        pl.when(has_high)(lambda: halo_up(pair).start())
        pl.when(has_low)(lambda: halo_down(pair).start())

    def await_halo(pair):
        pl.when(has_low)(lambda: halo_up(pair).wait_recv())
        pl.when(has_high)(lambda: halo_down(pair).wait_recv())

    lane = lax.broadcasted_iota(jnp.int32, (STRIP, cols), 1)
    first, final = lane == 0, lane == cols - 1

    def conv_batch(batch):
        scales = []
        for i, (n, f, y) in enumerate(batch):
            prod = jnp.dot(
                ws[...], hid[n, f, y * chans : (y + 3) * chans, :], preferred_element_type=F32
            )
            squares = jnp.zeros((STRIP, cols), F32)
            for at in strips:
                left, mid, right = (
                    prod[q * chans + at.start : q * chans + at.stop] for q in range(3)
                )
                left = jnp.where(first, 0.0, pltpu.roll(left, 1, 1))
                right = jnp.where(final, 0.0, pltpu.roll(right, cols - 1, 1))
                values = mid + left + right
                spat[i, at, :] = values
                squares += values * values
            scales.append(inverse_rms(squares, chans))
        for i, (n, f, y) in enumerate(batch):
            for at in strips:
                u = spat[i, at, :] * scales[i] * g2[at, :]
                low = (f + 2) * chans + at.start
                ext[n, y, low : low + STRIP, :] = silu_of_half(u)

    blocks = [(1, rows - 2), (0, 1), (rows - 1, 1)]

    def tail(off, piece):
        k, (low, size) = piece % 2, blocks[piece // 2]
        return pltpu.make_async_remote_copy(
            src_ref=send.at[off - 1, k, pl.ds(low, size)],
            dst_ref=recv.at[off - 1, k, pl.ds(low, size)],
            send_sem=tail_send.at[off - 1, piece],
            recv_sem=tail_recv.at[off - 1, piece],
            device_id={"group": lax.rem(me + off, group_count)},
            device_id_type=pl.DeviceIdType.MESH,
        )

    def send_tails(piece):
        k, (low, size) = piece % 2, blocks[piece // 2]
        f = frame_count - 2 + k
        at = slice((f + 2) * chans, (f + 3) * chans)
        for off in range(1, group_count):
            dest = lax.rem(me + off, group_count)
            wanted = jnp.int32(0)
            for n in range(slots):
                entry = dest * slots + n
                match = (packing[0, entry] > 0) & (packing[2, entry] == me)
                wanted = jnp.where(match, packing[3, entry], wanted)
            for y in range(low, low + size):
                value = ext[0, y, at, :]
                for n in range(1, slots):
                    value = lax.select(wanted == n, ext[n, y, at, :], value)
                send[off - 1, k, y] = value
            tail(off, piece).start()

    def temporal(n, y, pair):
        prod = jnp.dot(
            wt[...],
            ext[n, y, 2 * pair * chans : (2 * pair + 4) * chans, :],
            preferred_element_type=F32,
        )
        count = packing[1, me * slots + n]
        for k in range(2):
            f = 2 * pair + k
            value = x[n, f, y].astype(F32) + prod[k * chans : (k + 1) * chans]
            out[n, f, y] = lax.select(f < count, value, jnp.zeros_like(value)).astype(BF16)

    def tail_rows(piece, norms):
        k, (low, size) = piece % 2, blocks[piece // 2]

        conv_batch(
            [(n, frame_count - 2 + k, y) for n in range(slots) for y in range(low, low + size)]
        )
        for n in range(slots):
            for f in norms:
                norm_frame(n, f, range(rows))
        send_tails(piece)

    last = pairs - 1
    for copy in small[:4]:
        copy.wait()
    g1[...] = expand_gain(gain_one)
    g2[...] = expand_gain(gain_two)
    for q in range(3):
        ws[q * chans : (q + 1) * chans, :] = jnp.concatenate(
            [w_space[p, q] for p in range(3)], axis=1
        )
    fetch(last).wait()
    norm_slots(frame_count - 2, range(rows))
    pl.semaphore_wait(
        barrier, group_count - 1 + has_low.astype(jnp.int32) + has_high.astype(jnp.int32)
    )
    tail_rows(0, [])
    norm_slots(frame_count - 1, range(rows))
    send_halo(last)
    fetch(0).wait()
    tail_rows(1, [0, 1])
    send_halo(0)
    small[4].wait()
    zero = jnp.zeros((chans, chans), BF16)
    taps = [w_time[k] for k in range(3)]
    wt[0:chans, :] = jnp.concatenate(taps + [zero], axis=1)
    wt[chans : 2 * chans, :] = jnp.concatenate([zero] + taps, axis=1)
    await_halo(last)
    for pair in range(1, last):
        fetch(pair).wait()
    rest = list(range(2, frame_count - 2))
    share = -(-len(rest) // 4)
    for i in range(4):
        tail_rows(2 + i, rest[i * share : (i + 1) * share])
        for f in rest[i * share : (i + 1) * share]:
            if f % 2:
                send_halo(f // 2)
    for pair in range(pairs):
        if pair < last:
            await_halo(pair)

        def step(n, carry):
            if pair < last:
                conv_batch([(n, 2 * pair + k, y) for k in range(2) for y in range(rows)])
            if pair > 0:
                for y in range(rows):
                    temporal(n, y, pair)
            return carry

        lax.fori_loop(0, slots, step, 0)

    for block, (low, size) in enumerate(blocks):
        for off in range(1, group_count):
            for k in range(2):
                tail(off, 2 * block + k).wait_recv()

        def first_step(n, carry):
            entry = me * slots + n
            has_prev, source, slot = packing[0, entry] > 0, packing[2, entry], packing[3, entry]
            for y in range(low, low + size):
                for k in range(2):
                    at = slice((frame_count + k) * chans, (frame_count + k + 1) * chans)
                    value = jnp.zeros((chans, cols), BF16)
                    for s in range(slots):
                        own = has_prev & (source == me) & (slot == s)
                        value = lax.select(own, ext[s, y, at, :], value)
                    for off in range(1, group_count):
                        sender = lax.rem(me + group_count - off, group_count)
                        theirs = has_prev & (source == sender)
                        value = lax.select(theirs, recv[off - 1, k, y], value)
                    ext[n, y, k * chans : (k + 1) * chans, :] = value
                temporal(n, y, 0)
            return carry

        lax.fori_loop(0, slots, first_step, 0)

    for off in range(1, group_count):
        for piece in range(6):
            tail(off, piece).wait_send()
    for pair in range(pairs):
        pl.when(has_high)(lambda: halo_up(pair).wait_send())
        pl.when(has_low)(lambda: halo_down(pair).wait_send())


def body(group_count, frames, packing, w_space, w_time, gain_one, gain_two):
    slots, frame_count, rows, chans, cols = frames.shape
    pairs = frame_count // 2
    pixels = slots * frame_count * rows * cols
    return pl.pallas_call(
        kernel,
        out_shape=pltpu.VMEM(frames.shape, BF16),
        in_specs=[
            pl.BlockSpec(memory_space=pltpu.HBM) for _ in range(6)
        ],
        out_specs=pl.BlockSpec(memory_space=pltpu.VMEM),
        scratch_shapes=[
            pltpu.SMEM(packing.shape[::-1], jnp.int32),
            pltpu.VMEM(w_space.shape, BF16),
            pltpu.VMEM(w_time.shape, BF16),
            pltpu.VMEM((1, chans), F32),
            pltpu.VMEM((1, chans), F32),
            pltpu.VMEM(frames.shape, BF16),
            pltpu.VMEM((slots, frame_count, (rows + 2) * chans, cols), BF16),
            pltpu.VMEM((slots, rows, (frame_count + 2) * chans, cols), BF16),
            pltpu.VMEM((group_count - 1, 2, rows, chans, cols), BF16),
            pltpu.VMEM((group_count - 1, 2, rows, chans, cols), BF16),
            pltpu.VMEM((3 * chans, 3 * chans), BF16),
            pltpu.VMEM((2 * chans, 4 * chans), BF16),
            pltpu.VMEM((chans, cols), F32),
            pltpu.VMEM((chans, cols), F32),
            pltpu.VMEM((max(slots, 2) * rows, chans, cols), F32),
            pltpu.SemaphoreType.DMA((pairs,)),
            pltpu.SemaphoreType.DMA((5,)),
            pltpu.SemaphoreType.DMA((2, pairs)),
            pltpu.SemaphoreType.DMA((2, pairs)),
            pltpu.SemaphoreType.DMA((group_count - 1, 6)),
            pltpu.SemaphoreType.DMA((group_count - 1, 6)),
        ],
        cost_estimate=pl.CostEstimate(
            flops=24 * chans * chans * pixels,
            bytes_accessed=4 * chans * pixels,
            transcendentals=2 * chans * pixels,
        ),
        compiler_params=pltpu.CompilerParams(
            collective_id=0, has_side_effects=True, vmem_limit_bytes=54 * 1024 * 1024
        ),
    )(packing.T, frames, w_space, w_time, gain_one[None, :], gain_two[None, :])


def solution(mesh):
    in_specs = (P("group", None, "tile", None, None), P(), P(), P(), P(), P())
    out_specs = P("group", None, "tile", None, None)
    return jax.shard_map(
        functools.partial(body, mesh.shape["group"]),
        mesh=mesh, in_specs=in_specs, out_specs=out_specs, check_vma=False,
    )
```

```python
import functools

import jax
import jax.numpy as jnp
from jax import lax
from jax.experimental import pallas as pl
from jax.experimental.pallas import tpu as pltpu
from jax.sharding import PartitionSpec as P

BF16 = jnp.bfloat16
F32 = jnp.float32


STRIP = 16
LANES = 128


def silu_of_half(u):
    return (u + u * jnp.tanh(u)).astype(BF16)


def inverse_rms(squares, chans):
    return lax.rsqrt(jnp.sum(squares, axis=0, keepdims=True) * (1.0 / chans) + 1e-06)


def kernel(
    packing_hbm, frames_hbm, w_space_hbm, w_time_hbm, gain_one_hbm, gain_two_hbm, out,
    packing, w_space, w_time, gain_one, gain_two,
    x, hid, ext, send, recv, ws, wt, g1, g2, spat,
    in_sem, small_sem, halo_send, halo_recv, tail_send, tail_recv,
):
    slots, frame_count, rows, chans, cols = x.shape
    pairs = frame_count // 2
    group_count, tile_count = lax.axis_size("group"), lax.axis_size("tile")
    me, tile = lax.axis_index("group"), lax.axis_index("tile")
    has_low, has_high = tile > 0, tile < tile_count - 1
    order = [pairs - 1] + list(range(pairs - 1))

    def fetch(pair):
        return pltpu.make_async_copy(
            frames_hbm.at[:, pl.ds(2 * pair, 2)], x.at[:, pl.ds(2 * pair, 2)], in_sem.at[pair]
        )

    small = [
        pltpu.make_async_copy(src, dst, small_sem.at[i])
        for i, (src, dst) in enumerate(
            [
                (gain_one_hbm, gain_one), (packing_hbm, packing), (w_space_hbm, w_space),
                (gain_two_hbm, gain_two), (w_time_hbm, w_time),
            ]
        )
    ]
    for copy in small[:4]:
        copy.start()
    for pair in order:
        fetch(pair).start()
    small[4].start()

    barrier = pltpu.get_barrier_semaphore()
    for off in range(1, group_count):
        pl.semaphore_signal(
            barrier, inc=1, device_id={"group": lax.rem(me + off, group_count)},
            device_id_type=pl.DeviceIdType.MESH,
        )

    @pl.when(has_low)
    def _():
        pl.semaphore_signal(
            barrier, inc=1, device_id={"tile": tile - 1}, device_id_type=pl.DeviceIdType.MESH
        )

    @pl.when(has_high)
    def _():
        pl.semaphore_signal(
            barrier, inc=1, device_id={"tile": tile + 1}, device_id_type=pl.DeviceIdType.MESH
        )

    def expand_gain(gain):
        return jnp.transpose(jnp.broadcast_to(gain[...] * 0.5, (cols, chans)))

    @pl.when(tile == 0)
    def _():
        hid[:, :, 0:chans, :] = jnp.zeros((slots, frame_count, chans, cols), BF16)

    @pl.when(tile == tile_count - 1)
    def _():
        hid[:, :, (rows + 1) * chans :, :] = jnp.zeros((slots, frame_count, chans, cols), BF16)

    def halo_up(pair):
        at = pl.ds(2 * pair, 2)
        return pltpu.make_async_remote_copy(
            src_ref=hid.at[:, at, pl.ds(rows * chans, chans)],
            dst_ref=hid.at[:, at, pl.ds(0, chans)],
            send_sem=halo_send.at[0, pair],
            recv_sem=halo_recv.at[0, pair],
            device_id={"tile": lax.rem(tile + 1, tile_count)},
            device_id_type=pl.DeviceIdType.MESH,
        )

    def halo_down(pair):
        at = pl.ds(2 * pair, 2)
        return pltpu.make_async_remote_copy(
            src_ref=hid.at[:, at, pl.ds(chans, chans)],
            dst_ref=hid.at[:, at, pl.ds((rows + 1) * chans, chans)],
            send_sem=halo_send.at[1, pair],
            recv_sem=halo_recv.at[1, pair],
            device_id={"tile": lax.rem(tile + tile_count - 1, tile_count)},
            device_id_type=pl.DeviceIdType.MESH,
        )

    strips = [slice(low, low + STRIP) for low in range(0, chans, STRIP)]

    def norm_frame(n, f, which):
        scales = {}
        for y in which:
            squares = jnp.zeros((STRIP, cols), F32)
            for at in strips:
                values = x[n, f, y, at, :].astype(F32)
                squares += values * values
            scales[y] = inverse_rms(squares, chans)
        for y in which:
            for at in strips:
                u = x[n, f, y, at, :].astype(F32) * scales[y] * g1[at, :]
                low = (y + 1) * chans + at.start
                hid[n, f, low : low + STRIP, :] = silu_of_half(u)

    def norm_slots(f, which):
        def step(n, carry):
            norm_frame(n, f, which)
            return carry

        lax.fori_loop(0, slots, step, 0)

    def send_halo(pair):
        pl.when(has_high)(lambda: halo_up(pair).start())
        pl.when(has_low)(lambda: halo_down(pair).start())

    def await_halo(pair):
        pl.when(has_low)(lambda: halo_up(pair).wait_recv())
        pl.when(has_high)(lambda: halo_down(pair).wait_recv())

    lane = lax.broadcasted_iota(jnp.int32, (STRIP, LANES), 1)
    first, final = lane == 0, lane == LANES - 1
    spans = [slice(low, low + LANES) for low in range(0, cols, LANES)]
    empty = jnp.zeros((STRIP, LANES), F32)

    def shifted(pieces, step, edge):
        turned = [pltpu.roll(piece, step % LANES, 1) for piece in pieces]
        padded = [empty] + turned + [empty]
        return [jnp.where(edge, padded[i + 1 - step], turned[i]) for i in range(len(turned))]

    def conv_batch(batch):
        scales = []
        for i, (n, f, y) in enumerate(batch):
            prod = jnp.dot(
                ws[...], hid[n, f, y * chans : (y + 3) * chans, :], preferred_element_type=F32
            )
            squares = [empty] * len(spans)
            for at in strips:
                left, mid, right = (
                    [prod[q * chans + at.start : q * chans + at.stop, span] for span in spans]
                    for q in range(3)
                )
                left, right = shifted(left, 1, first), shifted(right, -1, final)
                for j, span in enumerate(spans):
                    values = mid[j] + left[j] + right[j]
                    spat[i, at, span] = values
                    squares[j] += values * values
            scales.append(jnp.concatenate([inverse_rms(part, chans) for part in squares], axis=1))
        for i, (n, f, y) in enumerate(batch):
            for at in strips:
                u = spat[i, at, :] * scales[i] * g2[at, :]
                low = (f + 2) * chans + at.start
                ext[n, y, low : low + STRIP, :] = silu_of_half(u)

    blocks = [(1, rows - 2), (0, 1), (rows - 1, 1)]

    def tail(off, piece):
        k, (low, size) = piece % 2, blocks[piece // 2]
        return pltpu.make_async_remote_copy(
            src_ref=send.at[off - 1, k, pl.ds(low, size)],
            dst_ref=recv.at[off - 1, k, pl.ds(low, size)],
            send_sem=tail_send.at[off - 1, piece],
            recv_sem=tail_recv.at[off - 1, piece],
            device_id={"group": lax.rem(me + off, group_count)},
            device_id_type=pl.DeviceIdType.MESH,
        )

    def send_tails(piece, before_start=lambda: None):
        k, (low, size) = piece % 2, blocks[piece // 2]
        f = frame_count - 2 + k
        at = slice((f + 2) * chans, (f + 3) * chans)
        for off in range(1, group_count):
            dest = lax.rem(me + off, group_count)
            wanted = jnp.int32(0)
            for n in range(slots):
                entry = dest * slots + n
                match = (packing[0, entry] > 0) & (packing[2, entry] == me)
                wanted = jnp.where(match, packing[3, entry], wanted)
            for y in range(low, low + size):
                value = ext[0, y, at, :]
                for n in range(1, slots):
                    value = lax.select(wanted == n, ext[n, y, at, :], value)
                send[off - 1, k, y] = value
        before_start()
        for off in range(1, group_count):
            tail(off, piece).start()

    def temporal(n, y, pair):
        prod = jnp.dot(
            wt[...],
            ext[n, y, 2 * pair * chans : (2 * pair + 4) * chans, :],
            preferred_element_type=F32,
        )
        count = packing[1, me * slots + n]
        for k in range(2):
            f = 2 * pair + k
            value = x[n, f, y].astype(F32) + prod[k * chans : (k + 1) * chans]
            out[n, f, y] = lax.select(f < count, value, jnp.zeros_like(value)).astype(BF16)

    def tail_rows(piece, norms, before_start=lambda: None):
        k, (low, size) = piece % 2, blocks[piece // 2]

        conv_batch(
            [(n, frame_count - 2 + k, y) for n in range(slots) for y in range(low, low + size)]
        )
        for n in range(slots):
            for f in norms:
                norm_frame(n, f, range(rows))
        send_tails(piece, before_start)

    last = pairs - 1
    for copy in small[:4]:
        copy.wait()
    g1[...] = expand_gain(gain_one)
    g2[...] = expand_gain(gain_two)
    for q in range(3):
        ws[q * chans : (q + 1) * chans, :] = jnp.concatenate(
            [w_space[p, q] for p in range(3)], axis=1
        )
    fetch(last).wait()
    norm_slots(frame_count - 2, range(rows))
    expected = group_count - 1 + has_low.astype(jnp.int32) + has_high.astype(jnp.int32)
    tail_rows(0, [], lambda: pl.semaphore_wait(barrier, expected))
    norm_slots(frame_count - 1, range(rows))
    send_halo(last)
    fetch(0).wait()
    tail_rows(1, [0, 1])
    send_halo(0)
    small[4].wait()
    zero = jnp.zeros((chans, chans), BF16)
    taps = [w_time[k] for k in range(3)]
    wt[0:chans, :] = jnp.concatenate(taps + [zero], axis=1)
    wt[chans : 2 * chans, :] = jnp.concatenate([zero] + taps, axis=1)
    await_halo(last)
    for pair in range(1, last):
        fetch(pair).wait()
    rest = list(range(2, frame_count - 2))
    share = -(-len(rest) // 4)
    for i in range(4):
        tail_rows(2 + i, rest[i * share : (i + 1) * share])
        for f in rest[i * share : (i + 1) * share]:
            if f % 2:
                send_halo(f // 2)
    for pair in range(pairs):
        if pair < last:
            await_halo(pair)

        def step(n, carry):
            if pair < last:
                conv_batch([(n, 2 * pair + k, y) for k in range(2) for y in range(rows)])
            if pair > 0:
                for y in range(rows):
                    temporal(n, y, pair)
            return carry

        lax.fori_loop(0, slots, step, 0)

    for block, (low, size) in enumerate(blocks):
        for off in range(1, group_count):
            for k in range(2):
                tail(off, 2 * block + k).wait_recv()

        for n in range(slots):
            entry = me * slots + n
            has_prev, source, slot = packing[0, entry] > 0, packing[2, entry], packing[3, entry]
            for y in range(low, low + size):
                for k in range(2):
                    at = slice((frame_count + k) * chans, (frame_count + k + 1) * chans)
                    value = jnp.zeros((chans, cols), BF16)
                    for s in range(slots):
                        own = has_prev & (source == me) & (slot == s)
                        value = lax.select(own, ext[s, y, at, :], value)
                    for off in range(1, group_count):
                        sender = lax.rem(me + group_count - off, group_count)
                        theirs = has_prev & (source == sender)
                        value = lax.select(theirs, recv[off - 1, k, y], value)
                    ext[n, y, k * chans : (k + 1) * chans, :] = value
                temporal(n, y, 0)

    for off in range(1, group_count):
        for piece in range(6):
            tail(off, piece).wait_send()
    for pair in range(pairs):
        pl.when(has_high)(lambda: halo_up(pair).wait_send())
        pl.when(has_low)(lambda: halo_down(pair).wait_send())


def body(group_count, frames, packing, w_space, w_time, gain_one, gain_two):
    slots, frame_count, rows, chans, cols = frames.shape
    pairs = frame_count // 2
    pixels = slots * frame_count * rows * cols
    return pl.pallas_call(
        kernel,
        out_shape=pltpu.VMEM(frames.shape, BF16),
        in_specs=[
            pl.BlockSpec(memory_space=pltpu.HBM) for _ in range(6)
        ],
        out_specs=pl.BlockSpec(memory_space=pltpu.VMEM),
        scratch_shapes=[
            pltpu.SMEM(packing.shape[::-1], jnp.int32),
            pltpu.VMEM(w_space.shape, BF16),
            pltpu.VMEM(w_time.shape, BF16),
            pltpu.VMEM((1, chans), F32),
            pltpu.VMEM((1, chans), F32),
            pltpu.VMEM(frames.shape, BF16),
            pltpu.VMEM((slots, frame_count, (rows + 2) * chans, cols), BF16),
            pltpu.VMEM((slots, rows, (frame_count + 2) * chans, cols), BF16),
            pltpu.VMEM((group_count - 1, 2, rows, chans, cols), BF16),
            pltpu.VMEM((group_count - 1, 2, rows, chans, cols), BF16),
            pltpu.VMEM((3 * chans, 3 * chans), BF16),
            pltpu.VMEM((2 * chans, 4 * chans), BF16),
            pltpu.VMEM((chans, cols), F32),
            pltpu.VMEM((chans, cols), F32),
            pltpu.VMEM((max(slots, 2) * rows, chans, cols), F32),
            pltpu.SemaphoreType.DMA((pairs,)),
            pltpu.SemaphoreType.DMA((5,)),
            pltpu.SemaphoreType.DMA((2, pairs)),
            pltpu.SemaphoreType.DMA((2, pairs)),
            pltpu.SemaphoreType.DMA((group_count - 1, 6)),
            pltpu.SemaphoreType.DMA((group_count - 1, 6)),
        ],
        cost_estimate=pl.CostEstimate(
            flops=24 * chans * chans * pixels,
            bytes_accessed=4 * chans * pixels,
            transcendentals=2 * chans * pixels,
        ),
        compiler_params=pltpu.CompilerParams(
            collective_id=0, has_side_effects=True, vmem_limit_bytes=54 * 1024 * 1024
        ),
    )(packing.T, frames, w_space, w_time, gain_one[None, :], gain_two[None, :])


def solution(mesh):
    in_specs = (P("group", None, "tile", None, None), P(), P(), P(), P(), P())
    out_specs = P("group", None, "tile", None, None)
    return jax.shard_map(
        functools.partial(body, mesh.shape["group"]),
        mesh=mesh, in_specs=in_specs, out_specs=out_specs, check_vma=False,
    )
```

```python
import functools

import jax
import jax.numpy as jnp
from jax import lax
from jax.experimental import pallas as pl
from jax.experimental.pallas import tpu as pltpu
from jax.sharding import PartitionSpec as P

BF16 = jnp.bfloat16
F32 = jnp.float32


STRIP = 16
LANES = 128


def silu_of_half(u):
    return (u + u * jnp.tanh(u)).astype(BF16)


def inverse_rms(squares, chans):
    return lax.rsqrt(jnp.sum(squares, axis=0, keepdims=True) * (1.0 / chans) + 1e-06)


def kernel(
    packing_hbm, frames_hbm, w_space_hbm, w_time_hbm, gain_one_hbm, gain_two_hbm, out,
    packing, w_space, w_time, gain_one, gain_two,
    x, hid, ext, send, recv, ws, wt, g1, g2, spat,
    in_sem, small_sem, halo_send, halo_recv, tail_send, tail_recv,
):
    slots, frame_count, rows, chans, cols = x.shape
    pairs = frame_count // 2
    group_count, tile_count = lax.axis_size("group"), lax.axis_size("tile")
    me, tile = lax.axis_index("group"), lax.axis_index("tile")
    has_low, has_high = tile > 0, tile < tile_count - 1
    order = [pairs - 1] + list(range(pairs - 1))

    def fetch(pair):
        return pltpu.make_async_copy(
            frames_hbm.at[:, pl.ds(2 * pair, 2)], x.at[:, pl.ds(2 * pair, 2)], in_sem.at[pair]
        )

    small = [
        pltpu.make_async_copy(src, dst, small_sem.at[i])
        for i, (src, dst) in enumerate(
            [
                (gain_one_hbm, gain_one), (packing_hbm, packing), (w_space_hbm, w_space),
                (gain_two_hbm, gain_two), (w_time_hbm, w_time),
            ]
        )
    ]
    for copy in small[:4]:
        copy.start()
    for pair in order:
        fetch(pair).start()
    small[4].start()

    barrier = pltpu.get_barrier_semaphore()
    for off in range(1, group_count):
        pl.semaphore_signal(
            barrier, inc=1, device_id={"group": lax.rem(me + off, group_count)},
            device_id_type=pl.DeviceIdType.MESH,
        )

    @pl.when(has_low)
    def _():
        pl.semaphore_signal(
            barrier, inc=1, device_id={"tile": tile - 1}, device_id_type=pl.DeviceIdType.MESH
        )

    @pl.when(has_high)
    def _():
        pl.semaphore_signal(
            barrier, inc=1, device_id={"tile": tile + 1}, device_id_type=pl.DeviceIdType.MESH
        )

    def expand_gain(gain):
        return jnp.transpose(jnp.broadcast_to(gain[...] * 0.5, (cols, chans)))

    @pl.when(tile == 0)
    def _():
        hid[:, :, 0:chans, :] = jnp.zeros((slots, frame_count, chans, cols), BF16)

    @pl.when(tile == tile_count - 1)
    def _():
        hid[:, :, (rows + 1) * chans :, :] = jnp.zeros((slots, frame_count, chans, cols), BF16)

    def halo_up(pair):
        at = pl.ds(2 * pair, 2)
        return pltpu.make_async_remote_copy(
            src_ref=hid.at[:, at, pl.ds(rows * chans, chans)],
            dst_ref=hid.at[:, at, pl.ds(0, chans)],
            send_sem=halo_send.at[0, pair],
            recv_sem=halo_recv.at[0, pair],
            device_id={"tile": lax.rem(tile + 1, tile_count)},
            device_id_type=pl.DeviceIdType.MESH,
        )

    def halo_down(pair):
        at = pl.ds(2 * pair, 2)
        return pltpu.make_async_remote_copy(
            src_ref=hid.at[:, at, pl.ds(chans, chans)],
            dst_ref=hid.at[:, at, pl.ds((rows + 1) * chans, chans)],
            send_sem=halo_send.at[1, pair],
            recv_sem=halo_recv.at[1, pair],
            device_id={"tile": lax.rem(tile + tile_count - 1, tile_count)},
            device_id_type=pl.DeviceIdType.MESH,
        )

    strips = [slice(low, low + STRIP) for low in range(0, chans, STRIP)]

    def norm_frame(n, f, which):
        scales = {}
        for y in which:
            squares = jnp.zeros((STRIP, cols), F32)
            for at in strips:
                values = x[n, f, y, at, :].astype(F32)
                squares += values * values
            scales[y] = inverse_rms(squares, chans)
        for y in which:
            for at in strips:
                u = x[n, f, y, at, :].astype(F32) * scales[y] * g1[at, :]
                low = (y + 1) * chans + at.start
                hid[n, f, low : low + STRIP, :] = silu_of_half(u)

    def norm_slots(f, which):
        for n in range(slots):
            norm_frame(n, f, which)

    def send_halo(pair):
        pl.when(has_high)(lambda: halo_up(pair).start())
        pl.when(has_low)(lambda: halo_down(pair).start())

    def await_halo(pair):
        pl.when(has_low)(lambda: halo_up(pair).wait_recv())
        pl.when(has_high)(lambda: halo_down(pair).wait_recv())

    lane = lax.broadcasted_iota(jnp.int32, (STRIP, LANES), 1)
    first, final = lane == 0, lane == LANES - 1
    spans = [slice(low, low + LANES) for low in range(0, cols, LANES)]
    empty = jnp.zeros((STRIP, LANES), F32)

    def shifted(pieces, step, edge):
        turned = [pltpu.roll(piece, step % LANES, 1) for piece in pieces]
        padded = [empty] + turned + [empty]
        return [jnp.where(edge, padded[i + 1 - step], turned[i]) for i in range(len(turned))]

    def conv_batch(batch):
        scales = []
        for i, (n, f, y) in enumerate(batch):
            prod = jnp.dot(
                ws[...], hid[n, f, y * chans : (y + 3) * chans, :], preferred_element_type=F32
            )
            squares = [empty] * len(spans)
            for at in strips:
                left, mid, right = (
                    [prod[q * chans + at.start : q * chans + at.stop, span] for span in spans]
                    for q in range(3)
                )
                left, right = shifted(left, 1, first), shifted(right, -1, final)
                for j, span in enumerate(spans):
                    values = mid[j] + left[j] + right[j]
                    spat[i, at, span] = values
                    squares[j] += values * values
            scales.append(jnp.concatenate([inverse_rms(part, chans) for part in squares], axis=1))
        for i, (n, f, y) in enumerate(batch):
            for at in strips:
                u = spat[i, at, :] * scales[i] * g2[at, :]
                low = (f + 2) * chans + at.start
                ext[n, y, low : low + STRIP, :] = silu_of_half(u)

    blocks = [(1, rows - 2), (0, 1), (rows - 1, 1)]

    def tail(off, piece):
        k, (low, size) = piece % 2, blocks[piece // 2]
        return pltpu.make_async_remote_copy(
            src_ref=send.at[off - 1, k, pl.ds(low, size)],
            dst_ref=recv.at[off - 1, k, pl.ds(low, size)],
            send_sem=tail_send.at[off - 1, piece],
            recv_sem=tail_recv.at[off - 1, piece],
            device_id={"group": lax.rem(me + off, group_count)},
            device_id_type=pl.DeviceIdType.MESH,
        )

    def send_tails(piece, before_start=lambda: None):
        k, (low, size) = piece % 2, blocks[piece // 2]
        f = frame_count - 2 + k
        at = slice((f + 2) * chans, (f + 3) * chans)
        for off in range(1, group_count):
            dest = lax.rem(me + off, group_count)
            wanted = jnp.int32(0)
            for n in range(slots):
                entry = dest * slots + n
                match = (packing[0, entry] > 0) & (packing[2, entry] == me)
                wanted = jnp.where(match, packing[3, entry], wanted)
            for y in range(low, low + size):
                value = ext[0, y, at, :]
                for n in range(1, slots):
                    value = lax.select(wanted == n, ext[n, y, at, :], value)
                send[off - 1, k, y] = value
        before_start()
        for off in range(1, group_count):
            tail(off, piece).start()

    def temporal(n, y, pair):
        prod = jnp.dot(
            wt[...],
            ext[n, y, 2 * pair * chans : (2 * pair + 4) * chans, :],
            preferred_element_type=F32,
        )
        count = packing[1, me * slots + n]
        for k in range(2):
            f = 2 * pair + k
            value = x[n, f, y].astype(F32) + prod[k * chans : (k + 1) * chans]
            out[n, f, y] = lax.select(f < count, value, jnp.zeros_like(value)).astype(BF16)

    def tail_rows(piece, norms, before_start=lambda: None):
        k, (low, size) = piece % 2, blocks[piece // 2]

        conv_batch(
            [(n, frame_count - 2 + k, y) for n in range(slots) for y in range(low, low + size)]
        )
        for n in range(slots):
            for f in norms:
                norm_frame(n, f, range(rows))
        send_tails(piece, before_start)

    last = pairs - 1
    for copy in small[:4]:
        copy.wait()
    g1[...] = expand_gain(gain_one)
    g2[...] = expand_gain(gain_two)
    for q in range(3):
        ws[q * chans : (q + 1) * chans, :] = jnp.concatenate(
            [w_space[p, q] for p in range(3)], axis=1
        )
    fetch(last).wait()
    norm_slots(frame_count - 2, range(rows))
    expected = group_count - 1 + has_low.astype(jnp.int32) + has_high.astype(jnp.int32)
    tail_rows(0, [], lambda: pl.semaphore_wait(barrier, expected))
    norm_slots(frame_count - 1, range(rows))
    send_halo(last)
    fetch(0).wait()
    tail_rows(1, [0, 1])
    send_halo(0)
    small[4].wait()
    zero = jnp.zeros((chans, chans), BF16)
    taps = [w_time[k] for k in range(3)]
    wt[0:chans, :] = jnp.concatenate(taps + [zero], axis=1)
    wt[chans : 2 * chans, :] = jnp.concatenate([zero] + taps, axis=1)
    await_halo(last)
    for pair in range(1, last):
        fetch(pair).wait()
    rest = list(range(2, frame_count - 2))
    share = -(-len(rest) // 4)
    for i in range(4):
        tail_rows(2 + i, rest[i * share : (i + 1) * share])
        for f in rest[i * share : (i + 1) * share]:
            if f % 2:
                send_halo(f // 2)
    for pair in range(pairs):
        if pair < last:
            await_halo(pair)

        def step(n, carry):
            if pair < last:
                conv_batch([(n, 2 * pair + k, y) for k in range(2) for y in range(rows)])
            if pair > 0:
                for y in range(rows):
                    temporal(n, y, pair)
            return carry

        lax.fori_loop(0, slots, step, 0)

    for block, (low, size) in enumerate(blocks):
        for off in range(1, group_count):
            for k in range(2):
                tail(off, 2 * block + k).wait_recv()

        for n in range(slots):
            entry = me * slots + n
            has_prev, source, slot = packing[0, entry] > 0, packing[2, entry], packing[3, entry]
            for y in range(low, low + size):
                for k in range(2):
                    at = slice((frame_count + k) * chans, (frame_count + k + 1) * chans)
                    value = jnp.zeros((chans, cols), BF16)
                    for s in range(slots):
                        own = has_prev & (source == me) & (slot == s)
                        value = lax.select(own, ext[s, y, at, :], value)
                    for off in range(1, group_count):
                        sender = lax.rem(me + group_count - off, group_count)
                        theirs = has_prev & (source == sender)
                        value = lax.select(theirs, recv[off - 1, k, y], value)
                    ext[n, y, k * chans : (k + 1) * chans, :] = value
                temporal(n, y, 0)

    for off in range(1, group_count):
        for piece in range(6):
            tail(off, piece).wait_send()
    for pair in range(pairs):
        pl.when(has_high)(lambda: halo_up(pair).wait_send())
        pl.when(has_low)(lambda: halo_down(pair).wait_send())


def body(group_count, frames, packing, w_space, w_time, gain_one, gain_two):
    slots, frame_count, rows, chans, cols = frames.shape
    pairs = frame_count // 2
    pixels = slots * frame_count * rows * cols
    return pl.pallas_call(
        kernel,
        out_shape=pltpu.VMEM(frames.shape, BF16),
        in_specs=[
            pl.BlockSpec(memory_space=pltpu.HBM) for _ in range(6)
        ],
        out_specs=pl.BlockSpec(memory_space=pltpu.VMEM),
        scratch_shapes=[
            pltpu.SMEM(packing.shape[::-1], jnp.int32),
            pltpu.VMEM(w_space.shape, BF16),
            pltpu.VMEM(w_time.shape, BF16),
            pltpu.VMEM((1, chans), F32),
            pltpu.VMEM((1, chans), F32),
            pltpu.VMEM(frames.shape, BF16),
            pltpu.VMEM((slots, frame_count, (rows + 2) * chans, cols), BF16),
            pltpu.VMEM((slots, rows, (frame_count + 2) * chans, cols), BF16),
            pltpu.VMEM((group_count - 1, 2, rows, chans, cols), BF16),
            pltpu.VMEM((group_count - 1, 2, rows, chans, cols), BF16),
            pltpu.VMEM((3 * chans, 3 * chans), BF16),
            pltpu.VMEM((2 * chans, 4 * chans), BF16),
            pltpu.VMEM((chans, cols), F32),
            pltpu.VMEM((chans, cols), F32),
            pltpu.VMEM((max(slots, 2) * rows, chans, cols), F32),
            pltpu.SemaphoreType.DMA((pairs,)),
            pltpu.SemaphoreType.DMA((5,)),
            pltpu.SemaphoreType.DMA((2, pairs)),
            pltpu.SemaphoreType.DMA((2, pairs)),
            pltpu.SemaphoreType.DMA((group_count - 1, 6)),
            pltpu.SemaphoreType.DMA((group_count - 1, 6)),
        ],
        cost_estimate=pl.CostEstimate(
            flops=24 * chans * chans * pixels,
            bytes_accessed=4 * chans * pixels,
            transcendentals=2 * chans * pixels,
        ),
        compiler_params=pltpu.CompilerParams(
            collective_id=0, has_side_effects=True, vmem_limit_bytes=54 * 1024 * 1024
        ),
    )(packing.T, frames, w_space, w_time, gain_one[None, :], gain_two[None, :])


def solution(mesh):
    in_specs = (P("group", None, "tile", None, None), P(), P(), P(), P(), P())
    out_specs = P("group", None, "tile", None, None)
    return jax.shard_map(
        functools.partial(body, mesh.shape["group"]),
        mesh=mesh, in_specs=in_specs, out_specs=out_specs, check_vma=False,
    )
```
